32 devices in a mesh: parts: 2 (over x), store: 4 (over z), tensor: 4 (over y, core).
Axes of the slice: x: 2, y: 2, z: 4, core: 2. Of those that a mesh axis runs over, the one named last changes fastest.
Arguments:
- tokens: bfloat16 [4096, 8192], P(('parts', 'store'), 'tensor'), parts along dimension 0, may hold values from -6 to 6
- output_weight: bfloat16 [8192, 8192], P('tensor'), may hold values from -0.0625 to 0.0625
- adapter_down_maps: bfloat16 [48, 64, 8192], P('store', None, 'tensor'), may hold values from -0.0625 to 0.0625
- adapter_up_maps: bfloat16 [48, 64, 8192], P('store', None, 'tensor'), may hold values from -0.75 to 0.75
- row_adapter_index: int32 [4096], P(('parts', 'store')), parts along dimension 0, may hold values from 0 to 47, as said below
- store_row_index: int32 [96], P('parts'), parts along dimension 0, may hold values from 0 to 47, as said below
Outputs:
- mixed: bfloat16 [4096, 8192], P(('parts', 'store'), 'tensor'), parts along dimension 0
The draws below stay inside these ranges and needn't reach their ends.
There are 2 independent parts, one for each index of `parts`. The reference program is written for one: setup_inputs(seed, part) draws one part's arguments, and reference() takes and returns one part's arrays. A program takes and returns all parts, laid end to end along the dimension named above; an argument that names none is the same for every part. Nothing has to cross between parts.
Inputs may be any that keep to these rules, and one draw needn't show every extreme that they name: `row_adapter_index`: the rows of one store group use at most 4 distinct adapters held by any one store owner, and exactly 4 of some owner in every group; every group uses adapters of every owner. `store_row_index`: A permutation.
All inputs are finite; a program needn't handle non-finite values.
Results may differ from the reference program's by a relative error of at most 0.0047.
Values may be sent and summed in bfloat16 or wider, within the bound.
A program may use at most 192 MiB of HBM per device.

```python
import math
import jax
import jax.numpy as jnp
from jax import lax

MODEL_WIDTH = 8192
ADAPTER_RANK = 64
ROW_DEV = 512
ADP_DEV = 12
SLOTS = 4
TOKENS = 2048
ADAPTER_TOTAL = 48


def store_layout(key):
    inner = jax.random.fold_in(key, 11)
    return jax.random.permutation(inner, ADAPTER_TOTAL).astype(jnp.int32)


def draw_store_row_index(key, part):
    return store_layout(key)


def draw_row_adapter_index(key, part):
    slot_of = store_layout(key)
    id_of = jnp.argsort(slot_of, stable=True).astype(jnp.int32)
    key = jax.random.fold_in(key, 5)
    owners = ADAPTER_TOTAL // ADP_DEV
    groups = TOKENS // ROW_DEV
    keys = jax.random.split(key, 5)
    counts = jax.random.randint(keys[0], (groups, owners), 1, SLOTS + 1)
    fullest = jax.random.randint(keys[1], (groups,), 0, owners)
    counts = jnp.where(jnp.arange(owners)[None, :] == fullest[:, None], SLOTS, counts)
    scores = jax.random.randint(keys[2], (groups, owners, ADP_DEV), 0, 2 ** 20) * ADP_DEV + jnp.arange(ADP_DEV)[None, None, :]
    order = jnp.argsort(scores, axis=2)[:, :, :SLOTS]
    chosen = jnp.arange(owners)[None, :, None] * ADP_DEV + order
    valid = jnp.arange(SLOTS)[None, None, :] < counts[:, :, None]
    chosen = chosen.reshape(groups, owners * SLOTS)
    valid = valid.reshape(groups, owners * SLOTS)
    rank_key = (1 - valid.astype(jnp.int32)) * (owners * SLOTS) + jnp.arange(owners * SLOTS)[None, :]
    compact = jnp.take_along_axis(chosen, jnp.argsort(rank_key, axis=1), axis=1)
    live = jnp.sum(valid.astype(jnp.int32), axis=1)
    pick = jax.random.randint(keys[3], (groups, ROW_DEV), 0, 256)
    skewed = pick * pick * live[:, None] // 65536
    position = jnp.arange(ROW_DEV)[None, :]
    which = jnp.where(position < live[:, None], position, skewed)
    row_slots = jnp.take_along_axis(compact, which, axis=1)
    shuffle = jax.random.randint(keys[4], (groups, ROW_DEV), 0, 2 ** 20) * ROW_DEV + position
    row_slots = jnp.take_along_axis(row_slots, jnp.argsort(shuffle, axis=1), axis=1)
    return id_of[row_slots.reshape(TOKENS)].astype(jnp.int32)


def levels(own_key, shape, pieces, least, top_value):
    level, own = 1.0, jax.random.fold_in(own_key, 6)
    for dim, shards_of in pieces:
        heights = jnp.exp(jax.random.uniform(jax.random.fold_in(own, dim), (shards_of,), jnp.float32, least / len(pieces), top_value / len(pieces)))
        level = level * jnp.repeat(heights, shape[dim] // shards_of).reshape([-1 if axis == dim else 1 for axis in range(len(shape))])
    return level


def noise(own_key, dims, scale, reach, cuts=(), kind=jnp.bfloat16):
    factor_of = levels(own_key, dims, cuts, -0.22, 0.18) if cuts else 1.0
    result = jax.random.normal(own_key, dims, jnp.float32) * scale * factor_of
    return jnp.minimum(jnp.maximum(result, -reach), reach).astype(kind)


def setup_inputs(seed: int = 0, part: int = 0) -> dict:
    key_of = jax.random.split(jax.random.key(seed), 7)
    part_keys = jax.random.split(jax.random.fold_in(key_of[6], part), 7)
    return {
        "tokens": noise(part_keys[0], (TOKENS, MODEL_WIDTH), 1.0, 6.0, ((0, 4), (1, 4))),
        "output_weight": noise(key_of[1], (MODEL_WIDTH, MODEL_WIDTH), MODEL_WIDTH ** -0.5, 0.0625, ((0, 4),)),
        "adapter_down_maps": noise(key_of[2], (ADAPTER_TOTAL, ADAPTER_RANK, MODEL_WIDTH), MODEL_WIDTH ** -0.5, 0.0625, ((0, 4), (2, 4))),
        "adapter_up_maps": noise(key_of[3], (ADAPTER_TOTAL, ADAPTER_RANK, MODEL_WIDTH), ADAPTER_RANK ** -0.5, 0.75, ((0, 4), (2, 4))),
        "row_adapter_index": draw_row_adapter_index(jax.random.fold_in(jax.random.fold_in(key_of[6], part), 71), part),
        "store_row_index": draw_store_row_index(jax.random.fold_in(jax.random.fold_in(key_of[6], part), 71), part),
    }


adapter_scale = 2.0


def reference(tokens, output_weight, adapter_down_maps, adapter_up_maps, row_adapter_index, store_row_index):
    slots = store_row_index[row_adapter_index].astype(jnp.int32)
    base = jnp.dot(tokens, output_weight, preferred_element_type=jnp.float32)
    block = math.gcd(TOKENS, 128)
    tok_blocks = tokens.reshape(TOKENS // block, block, MODEL_WIDTH)
    slot_blocks = slots.reshape(TOKENS // block, block)

    def one_block(pair):
        batch_rows, selected_slots = pair
        down_map_rows = adapter_down_maps[selected_slots].astype(jnp.float32)
        down_product = jnp.einsum("pi,pgi->pg", batch_rows.astype(jnp.float32), down_map_rows)
        low_rank_state = (adapter_scale * down_product).astype(jnp.bfloat16)
        up_map_rows = adapter_up_maps[selected_slots].astype(jnp.float32)
        return jnp.einsum("op,opn->on", low_rank_state.astype(jnp.float32), up_map_rows)

    extra = lax.map(one_block, (tok_blocks, slot_blocks)).reshape(TOKENS, MODEL_WIDTH)
    return (base + extra).astype(jnp.bfloat16)
```

```python
import functools

import jax
import jax.numpy as jnp
from jax import lax
from jax.experimental import pallas as pl
from jax.experimental.pallas import tpu as pltpu
from jax.sharding import PartitionSpec as P

SLOTS = 4
CORES = 2
adapter_scale = 2.0
F32, BF16 = jnp.float32, jnp.bfloat16


def kernel(
    S, T, rank, tile,
    tok_hbm, w_hbm, a_hbm, b_hbm, want_ref, bidx_ref,
    out_ref,
    tok, a_own, b_own, send_a, send_b, got_a, got_b, got_want, want_s,
    wbuf, send1, got1, send2, got2, acc, down, got_down, lowm,
    in_sem, w_sem, want_local,
    want_ss, want_rs, a_ss, a_rs, b_ss, b_rs,
    s1_ss, s1_rs, s2_ss, s2_rs, d_ss, d_rs,
):
    Y = T // CORES
    here = lax.axis_index("store")
    mine = lax.axis_index("tensor")
    my_y, my_c = mine // CORES, mine % CORES
    rows, hidden = out_ref.shape
    width = SLOTS * rank

    def remote(src, dst, ssem, rsem, **where):
        return pltpu.make_async_remote_copy(
            src_ref=src, dst_ref=dst, send_sem=ssem, recv_sem=rsem,
            device_id=where, device_id_type=pl.DeviceIdType.MESH,
        )

    ins = [
        pltpu.make_async_copy(src, dst, in_sem.at[i])
        for i, (src, dst) in enumerate(((a_hbm, a_own), (b_hbm, b_own), (tok_hbm, tok)))
    ]
    for c in ins:
        c.start()

    barrier = pltpu.get_barrier_semaphore()
    for d in range(1, S):
        pl.semaphore_signal(
            barrier, inc=1, device_id={"store": lax.rem(here + d, S)},
            device_id_type=pl.DeviceIdType.MESH,
        )
    for d in range(1, T):
        pl.semaphore_signal(
            barrier, inc=1, device_id={"tensor": lax.rem(mine + d, T)},
            device_id_type=pl.DeviceIdType.MESH,
        )
    pl.semaphore_wait(barrier, S - 1 + T - 1)

    want_copies = []
    for d in range(1, S):
        to = lax.rem(here + d, S)
        c = remote(want_ref.at[to], got_want.at[d], want_ss.at[d], want_rs.at[d], store=to)
        c.start()
        want_copies.append(c)

    per_block = hidden // tile
    tiles = T * per_block

    def weight_copy(i, slot):
        block, sub = i // per_block, i % per_block
        y = lax.rem(my_y + 1 + block % Y, Y)
        core = jnp.where(block < Y, 1 - my_c, my_c)
        col = pl.multiple_of((y * CORES + core) * hidden + sub * tile, tile)
        return pltpu.make_async_copy(w_hbm.at[:, pl.ds(col, tile)], wbuf.at[slot], w_sem.at[slot])

    weight_copy(0, 0).start()

    order = list(range(1, S))
    local = []
    for d in order:
        want_copies[S - d - 1].wait_recv()
        c = pltpu.make_async_copy(got_want.at[S - d], want_s.at[d], want_local.at[d])
        c.start()
        local.append(c)
    c = pltpu.make_async_copy(want_ref.at[here], want_s.at[0], want_local.at[0])
    c.start()
    for x in local + [c]:
        x.wait()

    def fill(own, sends, d):
        for j in range(SLOTS):
            sends[d, j * rank:(j + 1) * rank, :] = own[want_s[d, 0, j]]

    ins[0].wait()
    a_copies, b_copies = {}, {}
    for d in order:
        fill(a_own, send_a, d)
        a_copies[d] = remote(
            send_a.at[d], got_a.at[d], a_ss.at[d], a_rs.at[d], store=lax.rem(here + d, S)
        )
        a_copies[d].start()
    ins[1].wait()
    for d in order:
        fill(b_own, send_b, d)
        b_copies[d] = remote(
            send_b.at[d], got_b.at[d], b_ss.at[d], b_rs.at[d], store=lax.rem(here + d, S)
        )
        b_copies[d].start()
    fill(a_own, send_a, 0)
    fill(b_own, send_b, 0)
    ins[2].wait()

    def product(i):
        slot = lax.rem(i, 2)

        @pl.when(i + 1 < tiles)
        def _():
            weight_copy(i + 1, 1 - slot).start()

        weight_copy(i, slot).wait()
        return jnp.dot(tok[...], wbuf[slot], preferred_element_type=F32)

    def cols(sub):
        return pl.ds(pl.multiple_of(sub * tile, tile), tile)

    s1, s2 = [], []
    for k in range(Y):

        @pl.loop(0, per_block)
        def _(sub, k=k):
            send1[k, :, cols(sub)] = product(k * per_block + sub).astype(BF16)

        c = remote(
            send1.at[k], got1.at[k], s1_ss.at[k], s1_rs.at[k],
            tensor=my_y * CORES + 1 - my_c,
        )
        c.start()
        s1.append(c)
    for k in range(Y):
        s1[k].wait_recv()

        @pl.loop(0, per_block)
        def _(sub, k=k):
            value = product((Y + k) * per_block + sub) + got1[k, :, cols(sub)].astype(F32)
            if k < Y - 1:
                send2[k, :, cols(sub)] = value.astype(BF16)
            else:
                acc[:, cols(sub)] = value

        if k < Y - 1:
            c = remote(
                send2.at[k], got2.at[k], s2_ss.at[k], s2_rs.at[k],
                tensor=lax.rem(my_y + 1 + k, Y) * CORES + my_c,
            )
            c.start()
            s2.append(c)

    bidx = bidx_ref[...]

    def owner_of(d):
        return lax.rem(here + S - d, S)

    total = jnp.zeros((rank, rows), F32)
    for d in range(S):
        if d:
            a_copies[d].wait_recv()
        maps = got_a[d] if d else send_a[0]
        part = lax.dot_general(maps, tok[...], (((1,), (1,)), ((), ())), preferred_element_type=F32)
        for j in range(SLOTS):
            total += jnp.where(
                bidx == owner_of(d) * SLOTS + j, part[j * rank:(j + 1) * rank, :], 0.0
            )
    down[...] = total
    dc = []
    for d in range(1, T):
        c = remote(
            down, got_down.at[d], d_ss.at[d], d_rs.at[d], tensor=lax.rem(mine + d, T)
        )
        c.start()
        dc.append(c)
    for c in s2:
        c.wait_recv()

    @pl.loop(0, per_block)
    def _(sub):
        value = acc[:, cols(sub)]
        for k in range(Y - 1):
            value += got2[k, :, cols(sub)].astype(F32)
        acc[:, cols(sub)] = value

    total = down[...]
    for d in range(1, T):
        dc[d - 1].wait_recv()
        total += got_down[d]
    low = (adapter_scale * total).astype(BF16).astype(F32)
    for d in range(S):
        lifted = jnp.concatenate(
            [jnp.where(bidx == owner_of(d) * SLOTS + j, low, 0.0) for j in range(SLOTS)], axis=0
        )
        lowm[d] = lifted.T.astype(BF16)

    for d in range(S):
        if d:
            b_copies[d].wait_recv()
        maps = got_b.at[d] if d else send_b.at[0]

        @pl.loop(0, per_block)
        def _(sub, d=d, maps=maps):
            value = acc[:, cols(sub)] + jnp.dot(
                lowm[d], maps[:, cols(sub)], preferred_element_type=F32
            )
            if d < S - 1:
                acc[:, cols(sub)] = value
            else:
                out_ref[:, cols(sub)] = value.astype(BF16)

    for c in want_copies + list(a_copies.values()) + list(b_copies.values()) + s1 + s2 + dc:
        c.wait_send()


def on_device(
    S, T,
    tokens, output_weight, adapter_down_maps, adapter_up_maps, row_adapter_index, store_row_index
):
    resident, rank, hidden = adapter_down_maps.shape
    rows = tokens.shape[0]
    count = store_row_index.shape[0]
    Y = T // CORES
    ids = jnp.arange(count, dtype=jnp.int32)

    own_slots = jnp.sum(
        jnp.where(row_adapter_index[None, :] == ids[:, None], store_row_index[:, None], 0), axis=0
    )
    hits = own_slots[None, :] == ids[:, None]
    used = jnp.any(hits, axis=1).astype(jnp.int32)
    earlier = (ids[None, :] < ids[:, None]) & (ids[None, :] // resident == ids[:, None] // resident)
    place = jnp.sum(jnp.where(earlier, used[None, :], 0), axis=1)
    buffer_of = ids // resident * SLOTS + place
    bidx = jnp.sum(jnp.where(hits, buffer_of[:, None], 0), axis=0, keepdims=True)
    lanes = jnp.arange(128, dtype=jnp.int32)
    owners = jnp.arange(S, dtype=jnp.int32)
    match = (
        (used[None, :, None] > 0)
        & (buffer_of[None, :, None] == owners[:, None, None] * SLOTS + lanes[None, None, :])
        & (lanes[None, None, :] < SLOTS)
    )
    want = jnp.sum(jnp.where(match, (ids % resident)[None, :, None], 0), axis=1)
    want = jnp.broadcast_to(want[:, None, :], (S, 8, 128)).astype(jnp.int32)

    width = SLOTS * rank
    tile = min(512, hidden)
    dma = pltpu.SemaphoreType.DMA
    any_, vmem = pl.BlockSpec(memory_space=pl.ANY), pl.BlockSpec(memory_space=pltpu.VMEM)
    flops = 2 * rows * hidden * hidden * T + 4 * rows * width * S * hidden
    return pl.pallas_call(
        functools.partial(kernel, S, T, rank, tile),
        out_shape=jax.ShapeDtypeStruct((rows, hidden), BF16),
        in_specs=[any_] * 4 + [vmem] * 2,
        out_specs=vmem,
        scratch_shapes=[
            pltpu.VMEM((rows, hidden), BF16),
            pltpu.VMEM((resident, rank, hidden), BF16),
            pltpu.VMEM((resident, rank, hidden), BF16),
            pltpu.VMEM((S, width, hidden), BF16),
            pltpu.VMEM((S, width, hidden), BF16),
            pltpu.VMEM((S, width, hidden), BF16),
            pltpu.VMEM((S, width, hidden), BF16),
            pltpu.VMEM((S, 8, 128), jnp.int32),
            pltpu.SMEM((S, 8, 128), jnp.int32),
            pltpu.VMEM((2, hidden, tile), BF16),
            pltpu.VMEM((Y, rows, hidden), BF16),
            pltpu.VMEM((Y, rows, hidden), BF16),
            pltpu.VMEM((max(Y - 1, 1), rows, hidden), BF16),
            pltpu.VMEM((max(Y - 1, 1), rows, hidden), BF16),
            pltpu.VMEM((rows, hidden), F32),
            pltpu.VMEM((rank, rows), F32),
            pltpu.VMEM((T, rank, rows), F32),
            pltpu.VMEM((S, rows, width), BF16),
            dma((3,)), dma((2,)), dma((S,)),
            dma((S,)), dma((S,)), dma((S,)), dma((S,)), dma((S,)), dma((S,)),
            dma((Y,)), dma((Y,)), dma((Y,)), dma((Y,)), dma((T,)), dma((T,)),
        ],
        compiler_params=pltpu.CompilerParams(
            collective_id=0, has_side_effects=True, vmem_limit_bytes=60 * 1024 * 1024
        ),
        cost_estimate=pl.CostEstimate(
            flops=flops, bytes_accessed=2 * hidden * hidden * T, transcendentals=0
        ),
    )(tokens, output_weight, adapter_down_maps, adapter_up_maps, want, bidx)


def solution(mesh):
    placed = (
        P(("parts", "store"), "tensor"),
        P("tensor", None),
        P("store", None, "tensor"),
        P("store", None, "tensor"),
        P(("parts", "store")),
        P("parts"),
    )
    return jax.shard_map(
        functools.partial(on_device, mesh.shape["store"], mesh.shape["tensor"]),
        mesh=mesh,
        in_specs=placed,
        out_specs=P(("parts", "store"), "tensor"),
        check_vma=False,
    )
```

```python
import functools

import jax
import jax.numpy as jnp
from jax import lax
from jax.experimental import pallas as pl
from jax.experimental.pallas import tpu as pltpu
from jax.sharding import PartitionSpec as P

SLOTS = 4
CORES = 2
CHUNKS = 4
UP_AFTER = 2
adapter_scale = 2.0
F32, BF16 = jnp.float32, jnp.bfloat16


def kernel(
    S, T, relay, rank, tile,
    tok_hbm, w_hbm, a_hbm, b_hbm, want_ref, bidx_ref,
    out_ref,
    tok, a_own, b_own, send_a, send_b, got_a, got_b, got_want, want_s,
    wbuf, send1, got1, send2, got2, acc, down, got_down, lowm,
    in_sem, w_sem, want_local,
    want_ss, want_rs, a_ss, a_rs, b_ss, b_rs,
    s1_ss, s1_rs, s2_ss, s2_rs, d_ss, d_rs,
    m_ss, m_rs, x_ss, x_rs, f_ss, f_rs, *crossed,
):
    Y = T // CORES
    here = lax.axis_index("store")
    mine = lax.axis_index("tensor")
    my_y, my_c = mine // CORES, mine % CORES
    rows, hidden = out_ref.shape
    width = SLOTS * rank

    def remote(src, dst, ssem, rsem, **where):
        return pltpu.make_async_remote_copy(
            src_ref=src, dst_ref=dst, send_sem=ssem, recv_sem=rsem,
            device_id=where, device_id_type=pl.DeviceIdType.MESH,
        )

    ins = [
        pltpu.make_async_copy(src, dst, in_sem.at[i])
        for i, (src, dst) in enumerate(((a_hbm, a_own), (b_hbm, b_own), (tok_hbm, tok)))
    ]
    for c in ins:
        c.start()

    barrier = pltpu.get_barrier_semaphore()
    for d in range(1, S):
        pl.semaphore_signal(
            barrier, inc=1, device_id={"store": lax.rem(here + d, S)},
            device_id_type=pl.DeviceIdType.MESH,
        )
    for d in range(1, T):
        pl.semaphore_signal(
            barrier, inc=1, device_id={"tensor": lax.rem(mine + d, T)},
            device_id_type=pl.DeviceIdType.MESH,
        )
    if relay:
        pl.semaphore_signal(
            barrier, inc=1, device_id={"parts": 1 - lax.axis_index("parts")},
            device_id_type=pl.DeviceIdType.MESH,
        )
    pl.semaphore_wait(barrier, S - 1 + T - 1 + int(relay))

    if relay:
        part = lax.axis_index("parts")
        half = here // 2
        inner = (here == 1) | (here == 2)
        nb = here + 1 - 2 * (here % 2)
        nb_d = lax.rem(nb - here + S, S)
        far = (2 - half, 3 * (1 - half))
        share = a_hbm.shape[0] // 2
        cw = hidden // CHUNKS
        mine_of = pl.ds(part * share, share)
        mid, swap, fwd = {}, {}, {}
        for k in range(2):
            for h in range(CHUNKS):
                at, hc = k * CHUNKS + h, pl.ds(h * cw, cw)
                mid[k, h] = remote(
                    a_hbm.at[mine_of, :, hc], crossed[at].at[mine_of], m_ss.at[h], m_rs.at[at],
                    store=2 - half,
                )
                swap[k, h] = remote(
                    crossed[at].at[mine_of], crossed[at].at[mine_of], x_ss.at[at], x_rs.at[at],
                    parts=1 - part,
                )
                fwd[k, h] = remote(
                    send_a.at[2 + k, :, hc], got_a.at[2 + k, :, hc], f_ss.at[at], f_rs.at[at],
                    store=nb,
                )

        @pl.when(inner)
        def _():
            for h in range(CHUNKS):
                mid[0, h].start()

        @pl.when(jnp.logical_not(inner))
        def _():
            for h in range(CHUNKS):
                mid[1, h].start()

    def relay_in(h):
        @pl.when(inner)
        def _():
            for k in range(2):
                mid[k, h].wait_recv()
                swap[k, h].start()

    def relay_out(h):
        @pl.when(inner)
        def _():
            for k in range(2):
                swap[k, h].wait_recv()
                ref = crossed[k * CHUNKS + h]
                hs = slice(h * cw, (h + 1) * cw)
                for j in range(SLOTS):
                    js = slice(j * rank, (j + 1) * rank)
                    send_a[2 + k, js, hs] = ref[want_s[nb_d, far[k], j]]
                fwd[k, h].start()
                for j in range(SLOTS):
                    js = slice(j * rank, (j + 1) * rank)
                    got_a[2 + k, js, hs] = ref[want_s[0, far[k], j]]

    want_copies = []
    for d in range(1, S):
        to = lax.rem(here + d, S)
        c = remote(want_ref, got_want.at[d], want_ss.at[d], want_rs.at[d], store=to)
        c.start()
        want_copies.append(c)

    per_block = hidden // tile
    tiles = T * per_block

    def weight_copy(i, slot):
        block, sub = i // per_block, i % per_block
        y = lax.rem(my_y + 1 + block % Y, Y)
        core = jnp.where(block < Y, 1 - my_c, my_c)
        col = pl.multiple_of((y * CORES + core) * hidden + sub * tile, tile)
        return pltpu.make_async_copy(w_hbm.at[:, pl.ds(col, tile)], wbuf.at[slot], w_sem.at[slot])

    weight_copy(0, 0).start()

    order = list(range(1, S))
    local = []
    for d in order:
        want_copies[S - d - 1].wait_recv()
        c = pltpu.make_async_copy(got_want.at[S - d], want_s.at[d], want_local.at[d])
        c.start()
        local.append(c)
    c = pltpu.make_async_copy(want_ref, want_s.at[0], want_local.at[0])
    c.start()
    for x in local + [c]:
        x.wait()

    def fill(own, sends, d, at=None):
        for j in range(SLOTS):
            sends[d if at is None else at, j * rank:(j + 1) * rank, :] = own[want_s[d, here, j]]

    ins[0].wait()
    a_copies, b_copies = {}, {}
    if relay:
        fill(a_own, send_a, nb_d, 1)
        a_copies[1] = remote(send_a.at[1], got_a.at[1], a_ss.at[1], a_rs.at[1], store=nb)
        a_copies[1].start()
    else:
        for d in order:
            fill(a_own, send_a, d)
            a_copies[d] = remote(
                send_a.at[d], got_a.at[d], a_ss.at[d], a_rs.at[d], store=lax.rem(here + d, S)
            )
            a_copies[d].start()

    def send_up():
        ins[1].wait()
        for d in order:
            fill(b_own, send_b, d)
            b_copies[d] = remote(
                send_b.at[d], got_b.at[d], b_ss.at[d], b_rs.at[d], store=lax.rem(here + d, S)
            )
            b_copies[d].start()
        fill(b_own, send_b, 0)

    if not relay:
        send_up()
    fill(a_own, send_a, 0)
    ins[2].wait()

    steps = []
    if relay:
        for h in range(CHUNKS):
            steps.append(functools.partial(relay_in, h))
            if h:
                steps.append(functools.partial(relay_out, h - 1))
            if h == UP_AFTER:
                steps.append(send_up)
        steps.append(functools.partial(relay_out, CHUNKS - 1))
    steps_per_block = 2

    def some_steps(last=False):
        for step in steps[:None if last else steps_per_block]:
            step()
        del steps[:None if last else steps_per_block]

    def product(i):
        slot = lax.rem(i, 2)

        @pl.when(i + 1 < tiles)
        def _():
            weight_copy(i + 1, 1 - slot).start()

        weight_copy(i, slot).wait()
        return jnp.dot(tok[...], wbuf[slot], preferred_element_type=F32)

    def cols(sub):
        return pl.ds(pl.multiple_of(sub * tile, tile), tile)

    s1, s2 = [], []
    for k in range(Y):

        @pl.loop(0, per_block)
        def _(sub, k=k):
            send1[k, :, cols(sub)] = product(k * per_block + sub).astype(BF16)

        c = remote(
            send1.at[k], got1.at[k], s1_ss.at[k], s1_rs.at[k],
            tensor=my_y * CORES + 1 - my_c,
        )
        c.start()
        s1.append(c)
        some_steps()
    for k in range(Y):
        s1[k].wait_recv()

        @pl.loop(0, per_block)
        def _(sub, k=k):
            value = product((Y + k) * per_block + sub) + got1[k, :, cols(sub)].astype(F32)
            if k < Y - 1:
                send2[k, :, cols(sub)] = value.astype(BF16)
            else:
                acc[:, cols(sub)] = value

        if k < Y - 1:
            c = remote(
                send2.at[k], got2.at[k], s2_ss.at[k], s2_rs.at[k],
                tensor=lax.rem(my_y + 1 + k, Y) * CORES + my_c,
            )
            c.start()
            s2.append(c)
        some_steps(k == Y - 1)

    bidx = bidx_ref[...]

    def owner_of(d):
        return lax.rem(here + S - d, S)

    total = jnp.zeros((rank, rows), F32)
    for d in range(S):
        owner = owner_of(d)
        if relay and d:
            owner = (nb, *far)[d - 1]
        if d and d in a_copies:
            a_copies[d].wait_recv()
        elif d:

            @pl.when(jnp.logical_not(inner))
            def _(d=d):
                for h in range(CHUNKS):
                    fwd[d - 2, h].wait_recv()

        maps = got_a[d] if d else send_a[0]
        piece = lax.dot_general(maps, tok[...], (((1,), (1,)), ((), ())), preferred_element_type=F32)
        for j in range(SLOTS):
            total += jnp.where(
                bidx == owner * SLOTS + j, piece[j * rank:(j + 1) * rank, :], 0.0
            )
    down[...] = total
    dc = []
    for d in range(1, T):
        c = remote(
            down, got_down.at[d], d_ss.at[d], d_rs.at[d], tensor=lax.rem(mine + d, T)
        )
        c.start()
        dc.append(c)
    for c in s2:
        c.wait_recv()

    @pl.loop(0, per_block)
    def _(sub):
        value = acc[:, cols(sub)]
        for k in range(Y - 1):
            value += got2[k, :, cols(sub)].astype(F32)
        acc[:, cols(sub)] = value

    total = down[...]
    for d in range(1, T):
        dc[d - 1].wait_recv()
        total += got_down[d]
    low = (adapter_scale * total).astype(BF16).astype(F32)
    for d in range(S):
        lifted = jnp.concatenate(
            [jnp.where(bidx == owner_of(d) * SLOTS + j, low, 0.0) for j in range(SLOTS)], axis=0
        )
        lowm[d] = lifted.T.astype(BF16)

    for d in range(S):
        if d:
            b_copies[d].wait_recv()
        maps = got_b.at[d] if d else send_b.at[0]

        @pl.loop(0, per_block)
        def _(sub, d=d, maps=maps):
            value = acc[:, cols(sub)] + jnp.dot(
                lowm[d], maps[:, cols(sub)], preferred_element_type=F32
            )
            if d < S - 1:
                acc[:, cols(sub)] = value
            else:
                out_ref[:, cols(sub)] = value.astype(BF16)

    for c in want_copies + list(a_copies.values()) + list(b_copies.values()) + s1 + s2 + dc:
        c.wait_send()
    if relay:
        for h in range(CHUNKS):
            mid[0, h].wait_send()

        @pl.when(inner)
        def _():
            for c in list(swap.values()) + list(fwd.values()):
                c.wait_send()


def on_device(
    S, T, parts,
    tokens, output_weight, adapter_down_maps, adapter_up_maps, row_adapter_index, store_row_index
):
    resident, rank, hidden = adapter_down_maps.shape
    rows = tokens.shape[0]
    count = store_row_index.shape[0]
    Y = T // CORES
    ids = jnp.arange(count, dtype=jnp.int32)

    own_slots = jnp.sum(
        jnp.where(row_adapter_index[None, :] == ids[:, None], store_row_index[:, None], 0), axis=0
    )
    hits = own_slots[None, :] == ids[:, None]
    used = jnp.any(hits, axis=1).astype(jnp.int32)
    earlier = (ids[None, :] < ids[:, None]) & (ids[None, :] // resident == ids[:, None] // resident)
    place = jnp.sum(jnp.where(earlier, used[None, :], 0), axis=1)
    buffer_of = ids // resident * SLOTS + place
    bidx = jnp.sum(jnp.where(hits, buffer_of[:, None], 0), axis=0, keepdims=True)
    lanes = jnp.arange(128, dtype=jnp.int32)
    owners = jnp.arange(S, dtype=jnp.int32)
    match = (
        (used[None, :, None] > 0)
        & (buffer_of[None, :, None] == owners[:, None, None] * SLOTS + lanes[None, None, :])
        & (lanes[None, None, :] < SLOTS)
    )
    want = jnp.sum(jnp.where(match, (ids % resident)[None, :, None], 0), axis=1)
    table = -(-S // 8) * 8
    want = jnp.pad(want, ((0, table - S), (0, 0))).astype(jnp.int32)

    width = SLOTS * rank
    tile = min(512, hidden)
    relay = S == 4 and parts == 2 and resident % 2 == 0 and hidden % (128 * CHUNKS) == 0
    both = 2 * CHUNKS
    crossed = [pltpu.VMEM((resident, rank, hidden // CHUNKS), BF16)] * (both if relay else 0)
    dma = pltpu.SemaphoreType.DMA
    any_, vmem = pl.BlockSpec(memory_space=pl.ANY), pl.BlockSpec(memory_space=pltpu.VMEM)
    flops = 2 * rows * hidden * hidden * T + 4 * rows * width * S * hidden
    return pl.pallas_call(
        functools.partial(kernel, S, T, relay, rank, tile),
        out_shape=jax.ShapeDtypeStruct((rows, hidden), BF16),
        in_specs=[any_] * 4 + [vmem] * 2,
        out_specs=vmem,
        scratch_shapes=[
            pltpu.VMEM((rows, hidden), BF16),
            pltpu.VMEM((resident, rank, hidden), BF16),
            pltpu.VMEM((resident, rank, hidden), BF16),
            pltpu.VMEM((S, width, hidden), BF16),
            pltpu.VMEM((S, width, hidden), BF16),
            pltpu.VMEM((S, width, hidden), BF16),
            pltpu.VMEM((S, width, hidden), BF16),
            pltpu.VMEM((S, table, 128), jnp.int32),
            pltpu.SMEM((S, table, 128), jnp.int32),
            pltpu.VMEM((2, hidden, tile), BF16),
            pltpu.VMEM((Y, rows, hidden), BF16),
            pltpu.VMEM((Y, rows, hidden), BF16),
            pltpu.VMEM((max(Y - 1, 1), rows, hidden), BF16),
            pltpu.VMEM((max(Y - 1, 1), rows, hidden), BF16),
            pltpu.VMEM((rows, hidden), F32),
            pltpu.VMEM((rank, rows), F32),
            pltpu.VMEM((T, rank, rows), F32),
            pltpu.VMEM((S, rows, width), BF16),
            dma((3,)), dma((2,)), dma((S,)),
            dma((S,)), dma((S,)), dma((S,)), dma((S,)), dma((S,)), dma((S,)),
            dma((Y,)), dma((Y,)), dma((Y,)), dma((Y,)), dma((T,)), dma((T,)),
            dma((CHUNKS,)), dma((both,)), dma((both,)), dma((both,)), dma((both,)), dma((both,)),
            *crossed,
        ],
        compiler_params=pltpu.CompilerParams(
            collective_id=0, has_side_effects=True, vmem_limit_bytes=60 * 1024 * 1024
        ),
        cost_estimate=pl.CostEstimate(
            flops=flops, bytes_accessed=2 * hidden * hidden * T, transcendentals=0
        ),
    )(tokens, output_weight, adapter_down_maps, adapter_up_maps, want, bidx)


def solution(mesh):
    placed = (
        P(("parts", "store"), "tensor"),
        P("tensor", None),
        P("store", None, "tensor"),
        P("store", None, "tensor"),
        P(("parts", "store")),
        P("parts"),
    )
    return jax.shard_map(
        functools.partial(on_device, mesh.shape["store"], mesh.shape["tensor"], mesh.shape["parts"]),
        mesh=mesh,
        in_specs=placed,
        out_specs=P(("parts", "store"), "tensor"),
        check_vma=False,
    )
```

```python
import functools

import jax
import jax.numpy as jnp
from jax import lax
from jax.experimental import pallas as pl
from jax.experimental.pallas import tpu as pltpu
from jax.sharding import PartitionSpec as P

SLOTS = 4
CORES = 2
adapter_scale = 2.0
F32, BF16 = jnp.float32, jnp.bfloat16


def kernel(
    S, T, rank, tile,
    tok_hbm, w_hbm, a_hbm, b_hbm, want_ref, bidx_ref,
    out_ref,
    tok, a_own, b_own, send_a, send_b, got_a, got_b, got_want, want_s,
    wbuf, send1, got1, send2, got2, acc, down, got_down, lowm,
    in_sem, w_sem, want_local,
    want_ss, want_rs, a_ss, a_rs, b_ss, b_rs,
    s1_ss, s1_rs, s2_ss, s2_rs, d_ss, d_rs,
    relay_a, relay_b, r_ss, r_rs, g_ss, g_rs,
):
    Y = T // CORES
    here = lax.axis_index("store")
    mine = lax.axis_index("tensor")
    my_y, my_c = mine // CORES, mine % CORES
    rows, hidden = out_ref.shape
    width = SLOTS * rank

    def remote(src, dst, ssem, rsem, **where):
        return pltpu.make_async_remote_copy(
            src_ref=src, dst_ref=dst, send_sem=ssem, recv_sem=rsem,
            device_id=where, device_id_type=pl.DeviceIdType.MESH,
        )

    ins = [
        pltpu.make_async_copy(src, dst, in_sem.at[i])
        for i, (src, dst) in enumerate(((a_hbm, a_own), (b_hbm, b_own), (tok_hbm, tok)))
    ]
    for c in ins:
        c.start()

    barrier = pltpu.get_barrier_semaphore()
    for d in range(1, S):
        pl.semaphore_signal(
            barrier, inc=1, device_id={"store": lax.rem(here + d, S)},
            device_id_type=pl.DeviceIdType.MESH,
        )
    for d in range(1, T):
        pl.semaphore_signal(
            barrier, inc=1, device_id={"tensor": lax.rem(mine + d, T)},
            device_id_type=pl.DeviceIdType.MESH,
        )
    pl.semaphore_wait(barrier, S - 1 + T - 1)

    want_copies = []
    for d in range(1, S):
        to = lax.rem(here + d, S)
        c = remote(want_ref.at[to], got_want.at[d], want_ss.at[d], want_rs.at[d], store=to)
        c.start()
        want_copies.append(c)

    per_block = hidden // tile
    tiles = T * per_block

    def weight_copy(i, slot):
        block, sub = i // per_block, i % per_block
        y = lax.rem(my_y + 1 + block % Y, Y)
        core = jnp.where(block < Y, 1 - my_c, my_c)
        col = pl.multiple_of((y * CORES + core) * hidden + sub * tile, tile)
        return pltpu.make_async_copy(w_hbm.at[:, pl.ds(col, tile)], wbuf.at[slot], w_sem.at[slot])

    weight_copy(0, 0).start()

    order = list(range(1, S))
    local = []
    for d in order:
        want_copies[S - d - 1].wait_recv()
        c = pltpu.make_async_copy(got_want.at[S - d], want_s.at[d], want_local.at[d])
        c.start()
        local.append(c)
    c = pltpu.make_async_copy(want_ref.at[here], want_s.at[0], want_local.at[0])
    c.start()
    for x in local + [c]:
        x.wait()

    hops, ons = [], []
    if S == 4:
        back, top = lax.rem(here + 3, 4), pl.ds(width // 2, width // 2)
        for i, (a, r, g) in enumerate(((send_a, relay_a, got_a), (send_b, relay_b, got_b))):
            hops.append(remote(a.at[2, top], r, r_ss.at[i], r_rs.at[i], store=back))
            ons.append(remote(r, g.at[2, top], g_ss.at[i], g_rs.at[i], store=back))

    def pass_on(i):
        if hops:
            hops[i].wait_recv()
            ons[i].start()

    def fill(own, sends, d):
        for j in range(SLOTS):
            sends[d, j * rank:(j + 1) * rank, :] = own[want_s[d, 0, j]]

    def part_of(d):
        return pl.ds(0, width // 2 if hops and d == 2 else width)

    ins[0].wait()
    a_copies, b_copies = {}, {}
    for d in order:
        fill(a_own, send_a, d)
        a_copies[d] = remote(
            send_a.at[d, part_of(d)], got_a.at[d, part_of(d)], a_ss.at[d], a_rs.at[d],
            store=lax.rem(here + d, S),
        )
        a_copies[d].start()
        if hops and d == 2:
            hops[0].start()
    ins[1].wait()
    for d in order:
        fill(b_own, send_b, d)
        b_copies[d] = remote(
            send_b.at[d, part_of(d)], got_b.at[d, part_of(d)], b_ss.at[d], b_rs.at[d],
            store=lax.rem(here + d, S),
        )
        b_copies[d].start()
        if hops and d == 2:
            hops[1].start()
    fill(a_own, send_a, 0)
    fill(b_own, send_b, 0)
    ins[2].wait()

    def product(i):
        slot = lax.rem(i, 2)

        @pl.when(i + 1 < tiles)
        def _():
            weight_copy(i + 1, 1 - slot).start()

        weight_copy(i, slot).wait()
        return jnp.dot(tok[...], wbuf[slot], preferred_element_type=F32)

    def cols(sub):
        return pl.ds(pl.multiple_of(sub * tile, tile), tile)

    s1, s2 = [], []
    for k in range(Y):

        @pl.loop(0, per_block)
        def _(sub, k=k):
            send1[k, :, cols(sub)] = product(k * per_block + sub).astype(BF16)

        c = remote(
            send1.at[k], got1.at[k], s1_ss.at[k], s1_rs.at[k],
            tensor=my_y * CORES + 1 - my_c,
        )
        c.start()
        s1.append(c)
    pass_on(0)
    for k in range(Y):
        s1[k].wait_recv()

        @pl.loop(0, per_block)
        def _(sub, k=k):
            value = product((Y + k) * per_block + sub) + got1[k, :, cols(sub)].astype(F32)
            if k < Y - 1:
                send2[k, :, cols(sub)] = value.astype(BF16)
            else:
                acc[:, cols(sub)] = value

        if k < Y - 1:
            c = remote(
                send2.at[k], got2.at[k], s2_ss.at[k], s2_rs.at[k],
                tensor=lax.rem(my_y + 1 + k, Y) * CORES + my_c,
            )
            c.start()
            s2.append(c)

    bidx = bidx_ref[...]

    def owner_of(d):
        return lax.rem(here + S - d, S)

    total = jnp.zeros((rank, rows), F32)
    for d in range(S):
        if d:
            a_copies[d].wait_recv()
            if hops and d == 2:
                ons[0].wait_recv()
        maps = got_a[d] if d else send_a[0]
        part = lax.dot_general(maps, tok[...], (((1,), (1,)), ((), ())), preferred_element_type=F32)
        for j in range(SLOTS):
            total += jnp.where(
                bidx == owner_of(d) * SLOTS + j, part[j * rank:(j + 1) * rank, :], 0.0
            )
    down[...] = total
    dc = []
    for d in range(1, T):
        c = remote(
            down, got_down.at[d], d_ss.at[d], d_rs.at[d], tensor=lax.rem(mine + d, T)
        )
        c.start()
        dc.append(c)
    pass_on(1)
    for c in s2:
        c.wait_recv()

    @pl.loop(0, per_block)
    def _(sub):
        value = acc[:, cols(sub)]
        for k in range(Y - 1):
            value += got2[k, :, cols(sub)].astype(F32)
        acc[:, cols(sub)] = value

    total = down[...]
    for d in range(1, T):
        dc[d - 1].wait_recv()
        total += got_down[d]
    low = (adapter_scale * total).astype(BF16).astype(F32)
    for d in range(S):
        lifted = jnp.concatenate(
            [jnp.where(bidx == owner_of(d) * SLOTS + j, low, 0.0) for j in range(SLOTS)], axis=0
        )
        lowm[d] = lifted.T.astype(BF16)

    for d in range(S):
        if d:
            b_copies[d].wait_recv()
            if hops and d == 2:
                ons[1].wait_recv()
        maps = got_b.at[d] if d else send_b.at[0]

        @pl.loop(0, per_block)
        def _(sub, d=d, maps=maps):
            value = acc[:, cols(sub)] + jnp.dot(
                lowm[d], maps[:, cols(sub)], preferred_element_type=F32
            )
            if d < S - 1:
                acc[:, cols(sub)] = value
            else:
                out_ref[:, cols(sub)] = value.astype(BF16)

    for c in want_copies + list(a_copies.values()) + list(b_copies.values()) + s1 + s2 + dc + hops + ons:
        c.wait_send()


def on_device(
    S, T,
    tokens, output_weight, adapter_down_maps, adapter_up_maps, row_adapter_index, store_row_index
):
    resident, rank, hidden = adapter_down_maps.shape
    rows = tokens.shape[0]
    count = store_row_index.shape[0]
    Y = T // CORES
    ids = jnp.arange(count, dtype=jnp.int32)

    own_slots = jnp.sum(
        jnp.where(row_adapter_index[None, :] == ids[:, None], store_row_index[:, None], 0), axis=0
    )
    hits = own_slots[None, :] == ids[:, None]
    used = jnp.any(hits, axis=1).astype(jnp.int32)
    earlier = (ids[None, :] < ids[:, None]) & (ids[None, :] // resident == ids[:, None] // resident)
    place = jnp.sum(jnp.where(earlier, used[None, :], 0), axis=1)
    buffer_of = ids // resident * SLOTS + place
    bidx = jnp.sum(jnp.where(hits, buffer_of[:, None], 0), axis=0, keepdims=True)
    lanes = jnp.arange(128, dtype=jnp.int32)
    owners = jnp.arange(S, dtype=jnp.int32)
    match = (
        (used[None, :, None] > 0)
        & (buffer_of[None, :, None] == owners[:, None, None] * SLOTS + lanes[None, None, :])
        & (lanes[None, None, :] < SLOTS)
    )
    want = jnp.sum(jnp.where(match, (ids % resident)[None, :, None], 0), axis=1)
    want = jnp.broadcast_to(want[:, None, :], (S, 8, 128)).astype(jnp.int32)

    width = SLOTS * rank
    tile = min(512, hidden)
    dma = pltpu.SemaphoreType.DMA
    any_, vmem = pl.BlockSpec(memory_space=pl.ANY), pl.BlockSpec(memory_space=pltpu.VMEM)
    flops = 2 * rows * hidden * hidden * T + 4 * rows * width * S * hidden
    return pl.pallas_call(
        functools.partial(kernel, S, T, rank, tile),
        out_shape=jax.ShapeDtypeStruct((rows, hidden), BF16),
        in_specs=[any_] * 4 + [vmem] * 2,
        out_specs=vmem,
        scratch_shapes=[
            pltpu.VMEM((rows, hidden), BF16),
            pltpu.VMEM((resident, rank, hidden), BF16),
            pltpu.VMEM((resident, rank, hidden), BF16),
            pltpu.VMEM((S, width, hidden), BF16),
            pltpu.VMEM((S, width, hidden), BF16),
            pltpu.VMEM((S, width, hidden), BF16),
            pltpu.VMEM((S, width, hidden), BF16),
            pltpu.VMEM((S, 8, 128), jnp.int32),
            pltpu.SMEM((S, 8, 128), jnp.int32),
            pltpu.VMEM((2, hidden, tile), BF16),
            pltpu.VMEM((Y, rows, hidden), BF16),
            pltpu.VMEM((Y, rows, hidden), BF16),
            pltpu.VMEM((max(Y - 1, 1), rows, hidden), BF16),
            pltpu.VMEM((max(Y - 1, 1), rows, hidden), BF16),
            pltpu.VMEM((rows, hidden), F32),
            pltpu.VMEM((rank, rows), F32),
            pltpu.VMEM((T, rank, rows), F32),
            pltpu.VMEM((S, rows, width), BF16),
            dma((3,)), dma((2,)), dma((S,)),
            dma((S,)), dma((S,)), dma((S,)), dma((S,)), dma((S,)), dma((S,)),
            dma((Y,)), dma((Y,)), dma((Y,)), dma((Y,)), dma((T,)), dma((T,)),
            pltpu.VMEM((width // 2, hidden), BF16),
            pltpu.VMEM((width // 2, hidden), BF16),
            dma((2,)), dma((2,)), dma((2,)), dma((2,)),
        ],
        compiler_params=pltpu.CompilerParams(
            collective_id=0, has_side_effects=True, vmem_limit_bytes=60 * 1024 * 1024
        ),
        cost_estimate=pl.CostEstimate(
            flops=flops, bytes_accessed=2 * hidden * hidden * T, transcendentals=0
        ),
    )(tokens, output_weight, adapter_down_maps, adapter_up_maps, want, bidx)


def solution(mesh):
    placed = (
        P(("parts", "store"), "tensor"),
        P("tensor", None),
        P("store", None, "tensor"),
        P("store", None, "tensor"),
        P(("parts", "store")),
        P("parts"),
    )
    return jax.shard_map(
        functools.partial(on_device, mesh.shape["store"], mesh.shape["tensor"]),
        mesh=mesh,
        in_specs=placed,
        out_specs=P(("parts", "store"), "tensor"),
        check_vma=False,
    )
```
